32 devices in a mesh: wide: 8 (over y, x, core), narrow: 4 (over z).
Axes of the slice: x: 2, y: 2, z: 4, core: 2. Of those that a mesh axis runs over, the one named last changes fastest.
Arguments:
- weights_in: float32 [16, 32, 64, 2, 8, 128], P('wide', 'narrow'), may hold values from -6 to 6
- medium_speed: float32 [8, 8], replicated, may hold values from 0.5 to 2
- target_order: int32 [64], replicated, may hold values from 0 to 63, each once
Outputs:
- weights_out: float32 [16, 64, 32, 2, 8, 128], P('wide', 'narrow')
The draws below stay inside these ranges and needn't reach their ends.
Inputs may be any that keep to these rules, and one draw needn't show every extreme that they name: `target_order`: a permutation of the 64 starting target boxes.
All inputs are finite; a program needn't handle non-finite values.
Results may differ from the reference program's by a relative error of at most 0.0003.
Values sent between devices are 32-bit elements; how exact they have to be, the bound alone decides.
A program may use at most 192 MiB of HBM per device.

```python
import jax
import jax.numpy as jnp
from jax import lax

PTS = 8
RHS = 16
TX = 8
TY = 8
SYH = 4
SX = 32
SY = 16
SH = 32
TB = 64


def block_scale(own_key, shape, shards, smallest, high):
    def one(axis_at, shards_of):
        draws = jax.random.uniform(jax.random.fold_in(jax.random.fold_in(own_key, 6), axis_at), (shards_of,), jnp.float32, smallest / len(shards), high / len(shards))
        return jnp.repeat(jnp.exp(draws), shape[axis_at] // shards_of).reshape((-1,) + (1,) * (len(shape) - axis_at - 1))

    gain = one(*shards[0])
    for cut in shards[1:]:
        gain = gain * one(*cut)
    return gain


def centred(stream_key, extent, width, limit, shards=(), kind=jnp.bfloat16):
    values = width * jax.random.normal(stream_key, extent, jnp.float32)
    if shards:
        values = values * block_scale(stream_key, extent, shards, -0.22, 0.18)
    return jnp.clip(values, -limit, limit).astype(kind)


def setup_inputs(seed: int = 0) -> dict:
    arg_keys = jax.random.split(jax.random.key(seed), 4)
    weights_in = centred(arg_keys[0], (16, SH, TB, 2, PTS, PTS * RHS), 1.0, 6.0, ((0, 8), (1, 4)), jnp.float32)
    medium_speed = jnp.clip(jax.random.uniform(arg_keys[1], (TX, TY), jnp.float32, 0.5, 2.0), 0.5, 2.0)
    target_order = jax.random.permutation(arg_keys[2], TB).astype(jnp.int32)
    return dict(weights_in=weights_in, medium_speed=medium_speed, target_order=target_order)


level_bits = (3, 2, 1, 0)
merges_across = (1, 1, 2, 2)
merges_down = (0, 1, 1, 2)

def cheb_nodes():
    counter = jnp.arange(8, dtype=jnp.float32)
    return 0.5 - 0.5 * jnp.cos(jnp.pi * (2.0 * counter + 1.0) / 16.0)

def lagrange_matrix(child_bit):
    node_set = cheb_nodes()
    points = (child_bit.astype(jnp.float32) + node_set) / 2.0
    differ = points[None, :, None] - node_set[None, None, :]
    spacing = node_set[:, None] - node_set[None, :]
    diagonal = jnp.eye(8, dtype=bool)
    factors = jnp.where(diagonal[:, None, :], 1.0, differ / jnp.where(diagonal, 1.0, spacing)[:, None, :])
    return jnp.prod(factors, axis=2)

def take_bit(number, position):
    return number >> position & 1

def phase_angles(step_index, box_code, target_bit, source_super, target_box, speed_rows, layout, child_bit):
    across_boxes, down_boxes, tiles_across, tiles_down, supers_down = layout
    own_bit = level_bits[step_index]
    shift_across = merges_across[step_index]
    shift_down = merges_down[step_index]
    chosen = box_code & 15 - (1 << own_bit) | target_bit << own_bit
    whole_across = 4 * (source_super // supers_down) + 2 * take_bit(box_code, 1) + take_bit(box_code, 3)
    whole_down = 4 * (source_super % supers_down) + 2 * take_bit(box_code, 0) + take_bit(box_code, 2)
    side_across = 2 ** shift_across / across_boxes
    side_down = 2 ** shift_down / down_boxes
    corner_across = (whole_across >> shift_across).astype(jnp.float32) * side_across
    corner_down = (whole_down >> shift_down).astype(jnp.float32) * side_down
    tile_across = target_box // tiles_down * 2 ** shift_across + (2 * take_bit(chosen, 3) + take_bit(chosen, 1) >> 2 - shift_across)
    tile_down = target_box % tiles_down * 2 ** shift_down + (2 * take_bit(chosen, 2) + take_bit(chosen, 0) >> 2 - shift_down)
    center_across = (tile_across.astype(jnp.float32) + 0.5) / (tiles_across * 2 ** shift_across)
    center_down = (tile_down.astype(jnp.float32) + 0.5) / (tiles_down * 2 ** shift_down)
    node_set = cheb_nodes()
    along_first = node_set
    along_second = node_set
    if child_bit is not None:
        halved = (child_bit.astype(jnp.float32) + node_set) / 2.0
        if step_index % 2 == 0:
            along_first = halved
        else:
            along_second = halved
    key_across = corner_across[..., None, None] + side_across * along_first[:, None]
    key_down = corner_down[..., None, None] + side_down * along_second[None, :]
    base_across = (corner_across + 0.5 * side_across)[..., None, None]
    base_down = (corner_down + 0.5 * side_down)[..., None, None]
    key_square = key_across * key_across + key_down * key_down
    base_square = base_across * base_across + base_down * base_down
    radial = (key_square - base_square) / (jnp.sqrt(key_square) + jnp.sqrt(base_square))
    wave_scale = jnp.pi * across_boxes / 2.0
    return wave_scale * (center_across[..., None, None] * (key_across - base_across) + center_down[..., None, None] * (key_down - base_down) + speed_rows[..., None, None] * radial)

def pull_child(weights, angles, step_index, child_bit):
    shaped = weights.reshape(weights.shape[:-3] + (2, 8, 8, 16))
    real_part = shaped[..., 0, :, :, :]
    imag_part = shaped[..., 1, :, :, :]
    cosine = jnp.cos(angles)[..., None]
    sine_part = jnp.sin(angles)[..., None]
    turned_real = real_part * cosine + imag_part * sine_part
    turned_imag = imag_part * cosine - real_part * sine_part
    stacked = jnp.stack([turned_real, turned_imag], axis=-4)
    matrix = lagrange_matrix(child_bit)
    if step_index % 2 == 0:
        moved = jnp.einsum('ab,...bcd->...acd', matrix, stacked, precision=lax.Precision.HIGHEST)
    else:
        moved = jnp.einsum('ab,...cbd->...cad', matrix, stacked, precision=lax.Precision.HIGHEST)
    return moved.reshape(weights.shape)

def push_parent(summed, angles):
    shaped = summed.reshape(summed.shape[:-3] + (2, 8, 8, 16))
    real_part = shaped[..., 0, :, :, :]
    imag_part = shaped[..., 1, :, :, :]
    cosine = jnp.cos(angles)[..., None]
    sine_part = jnp.sin(angles)[..., None]
    out_real = real_part * cosine - imag_part * sine_part
    out_imag = real_part * sine_part + imag_part * cosine
    return jnp.stack([out_real, out_imag], axis=-4).reshape(summed.shape)

def merge_local(weights, step_index, code_base, source_super, target_box, speed_rows, layout):
    code_count = weights.shape[0]
    own_bit = level_bits[step_index]
    low_span = 1 << own_bit
    high_span = code_count // (2 * low_span)
    trailing = weights.shape[1:-3]
    split_view = weights.reshape((high_span, 2, low_span) + weights.shape[1:])
    ones_tail = (1,) * len(trailing)
    high_index = jnp.arange(high_span, dtype=jnp.int32).reshape((high_span, 1) + ones_tail)
    low_index = jnp.arange(low_span, dtype=jnp.int32).reshape((1, low_span) + ones_tail)
    results = []
    for target_bit in (0, 1):
        target_value = jnp.asarray(target_bit, dtype=jnp.int32)
        summed = None
        for child in (0, 1):
            child_value = jnp.asarray(child, dtype=jnp.int32)
            box_code = code_base + high_index * (2 * low_span) + child * low_span + low_index
            angles = phase_angles(step_index, box_code, target_value, source_super, target_box, speed_rows, layout, child_value)
            term = pull_child(split_view[:, child], angles, step_index, child_value)
            summed = term if summed is None else summed + term
        parent_code = code_base + high_index * (2 * low_span) + low_index
        parent_angles = phase_angles(step_index, parent_code, target_value, source_super, target_box, speed_rows, layout, None)
        results.append(push_parent(summed, parent_angles))
    return jnp.stack(results, axis=1).reshape(weights.shape)

def reference(weights_in, medium_speed, target_order):
    layout = (SX, SY, TX, TY, SYH)
    speed_flat = medium_speed.reshape(-1)
    target_box = jnp.arange(TB, dtype=jnp.int32)

    def one_super(super_index):
        super_block = lax.dynamic_index_in_dim(weights_in, super_index, axis=1, keepdims=False)
        source_super = super_index.reshape(1)
        for step_index in range(4):
            super_block = merge_local(super_block, step_index, 0, source_super, target_box, speed_flat, layout)
        return jnp.take(super_block, target_order, axis=1)
    stacked = lax.map(one_super, jnp.arange(SH, dtype=jnp.int32))
    return jnp.transpose(stacked, (1, 2, 0, 3, 4, 5))
```

```python
import functools

import jax
import jax.numpy as jnp
import ml_dtypes
import numpy as np
from jax import lax
from jax.experimental import pallas as pl
from jax.experimental.pallas import tpu as pltpu
from jax.sharding import PartitionSpec as P

TX = 8
TY = 8
SYH = 4
SUPERS = 4

MESH = pl.DeviceIdType.MESH
level_bits = (3, 2, 1, 0)


def cheb_nodes():
    return 0.5 - 0.5 * np.cos(np.pi * (2.0 * np.arange(8) + 1.0) / 16.0)


def lagrange_matrix(child):
    nodes = cheb_nodes()
    points = (child + nodes) / 2.0
    matrix = np.ones((8, 8))
    for q in range(8):
        for m in range(8):
            if m != q:
                matrix[q] *= (points - nodes[m]) / (nodes[q] - nodes[m])
    return matrix


def level_matrix(level, across_boxes, high, target, child):
    nodes = cheb_nodes()
    merges = 1 + level // 2
    boxes = across_boxes if level % 2 == 0 else 4 * SYH
    tiles = TX if level % 2 == 0 else TY
    side = 2.0**merges / boxes
    if merges == 1:
        shift = (target - 0.5) / (2 * tiles)
    else:
        shift = (2 * high + target - 1.5) / (4 * tiles)
    wave = np.pi * across_boxes / 2.0 * shift * side
    parent = np.exp(1j * wave * (nodes - 0.5))
    inner = np.exp(-1j * wave * ((child + nodes) / 2.0 - 0.5))
    matrix = parent[:, None] * lagrange_matrix(child) * inner[None, :]
    return np.block([[matrix.real, -matrix.imag], [matrix.imag, matrix.real]])


def all_matrices(across_boxes):
    found = []
    for level in range(4):
        for high in range(1 if level < 2 else 2):
            for target in range(2):
                for child in range(2):
                    small = level_matrix(level, across_boxes, high, target, child)
                    if level % 2 == 0:
                        big = np.kron(np.eye(16), small)
                    else:
                        big = np.kron(small.T, np.eye(16))
                    first = big.astype(np.float32).astype(ml_dtypes.bfloat16)
                    rest = (big - first.astype(np.float64)).astype(np.float32)
                    found.append(np.stack([first, rest.astype(ml_dtypes.bfloat16)]))
    return np.stack(found)


def turned(turns):
    part = turns - jnp.floor(turns + 0.5)
    half = part * np.float32(np.pi)
    square = half * half
    sine = np.float32(-1.0 / 39916800.0)
    for value in (1.0 / 362880.0, -1.0 / 5040.0, 1.0 / 120.0, -1.0 / 6.0, 1.0):
        sine = sine * square + np.float32(value)
    sine = sine * half
    cosine = np.float32(1.0 / 479001600.0)
    for value in (-1.0 / 3628800.0, 1.0 / 40320.0, -1.0 / 720.0, 1.0 / 24.0, -0.5, 1.0):
        cosine = cosine * square + np.float32(value)
    return 1.0 - 2.0 * sine * sine, 2.0 * sine * cosine


def split_two(value):
    first = value.astype(jnp.bfloat16)
    return first, (value - first.astype(jnp.float32)).astype(jnp.bfloat16)


def dot(left, right):
    return jnp.dot(left, right, preferred_element_type=jnp.float32)


def kernel(
    sizes,
    order_ref,
    speed_ref,
    weights_ref,
    mats_ref,
    nodes_ref,
    out_ref,
    held,
    outgoing,
    arrived,
    send_sem,
    recv_sem,
    far_send,
    far_recv,
    own_sem,
):
    wide, narrow, codes, supers, slots = sizes
    partner_levels = wide.bit_length() - 1
    local_bits = codes.bit_length() - 1
    parts = supers // SUPERS
    chunks = slots * parts
    across_boxes = 8 * narrow
    boxes = narrow * codes * SUPERS
    wide_place = lax.axis_index("wide")
    narrow_place = lax.axis_index("narrow")

    def device_bit(level):
        return wide_place >> (level_bits[level] - local_bits) & 1

    def partner(level):
        step = 1 << (level_bits[level] - local_bits)
        return wide_place + step * (1 - 2 * device_bit(level))

    def matrix(level, target, child):
        if level < 2:
            place = 4 * level + 2 * target + child
        else:
            place = 8 * level - 8 + 4 * device_bit(level - 2) + 2 * target + child
        return mats_ref[place, 0], mats_ref[place, 1]

    def far(step):
        return lax.rem(narrow_place + step, narrow)

    barrier = pltpu.get_barrier_semaphore()
    for level in range(partner_levels):
        pl.semaphore_signal(
            barrier, inc=1, device_id={"wide": partner(level)}, device_id_type=MESH
        )
    for step in range(1, narrow):
        pl.semaphore_signal(barrier, inc=1, device_id={"narrow": far(step)}, device_id_type=MESH)
    pl.semaphore_wait(barrier, partner_levels + narrow - 1)

    def swap(level, k):
        return pltpu.make_async_remote_copy(
            src_ref=outgoing.at[k],
            dst_ref=arrived.at[level, k],
            send_sem=send_sem.at[level, k],
            recv_sem=recv_sem.at[level, k],
            device_id={"wide": partner(level)},
            device_id_type=MESH,
        )

    def place_of(k):
        return out_ref.at[
            :, k // parts, pl.ds(narrow_place * supers + lax.rem(k, parts) * SUPERS, SUPERS)
        ]

    def hand_over(step, k):
        return pltpu.make_async_remote_copy(
            src_ref=outgoing.at[k, far(step)],
            dst_ref=place_of(k),
            send_sem=far_send.at[step - 1, k],
            recv_sem=far_recv.at[step - 1, k],
            device_id={"narrow": far(step)},
            device_id_type=MESH,
        )

    def hand_own(k):
        return pltpu.make_async_copy(outgoing.at[k, narrow_place], place_of(k), own_sem.at[k])

    def target_of(slot):
        box = order_ref[slot]
        speed = speed_ref[box]
        center_across = ((box // TY).astype(jnp.float32) + 0.5) * np.float32(1.0 / TX)
        center_down = ((box % TY).astype(jnp.float32) + 0.5) * np.float32(1.0 / TY)
        return box, center_across, center_down, speed * np.float32(across_boxes / 4.0)

    def radial(k, index, offset_across, offset_down):
        place = narrow_place * supers + lax.rem(k, parts) * SUPERS + index
        corner_across = (4 * (place // SYH)).astype(jnp.float32)
        corner_down = (4 * (place % SYH)).astype(jnp.float32)
        unit_across = np.float32(1.0 / across_boxes)
        unit_down = np.float32(1.0 / (4 * SYH))
        first = (corner_across + offset_across) * unit_across
        second = (corner_down + offset_down) * unit_down
        base_first = jnp.full((8, 128), (corner_across + 2.0) * unit_across)
        base_second = jnp.full((8, 128), (corner_down + 2.0) * unit_down)
        square = first * first + second * second
        base = base_first * base_first + base_second * base_second
        return (square - base) / (jnp.sqrt(square) + jnp.sqrt(base))

    nodes_across = nodes_ref[0]
    nodes_down = nodes_ref[1]
    down_scale = np.float32(across_boxes / 4.0 / (4 * SYH))

    def along_first(value):
        rows = value.reshape(boxes * 16, 128)
        pieces = [rows[256 * n : 256 * n + 256] for n in range(boxes // 16)]
        return split_two(jnp.concatenate(pieces, axis=1))

    def first_product(split, pair):
        total = dot(pair[0], split[0]) + dot(pair[0], split[1]) + dot(pair[1], split[0])
        pieces = [total[:, 128 * n : 128 * n + 128] for n in range(boxes // 16)]
        return jnp.concatenate(pieces, axis=0).reshape(narrow, codes, SUPERS, 2, 8, 128)

    def along_second(value):
        count = value.shape[0] * value.shape[1] * value.shape[2] * 8
        real = value[:, :, :, 0].reshape(count, 128)
        imag = value[:, :, :, 1].reshape(count, 128)
        return split_two(jnp.concatenate([real, imag], axis=1))

    def second_product(split, pair):
        return dot(split[0], pair[0]) + dot(split[1], pair[0]) + dot(split[0], pair[1])

    def store(into, level, k, split, pair):
        if level % 2 == 0:
            into[k] = first_product(split, pair)
        else:
            total = second_product(split, pair)
            shape = (narrow, codes, SUPERS, 8, 128)
            into[k, :, :, :, 0] = total[:, :128].reshape(shape)
            into[k, :, :, :, 1] = total[:, 128:].reshape(shape)

    def exchange(level, k, value):
        bit = device_bit(level)
        split = along_first(value) if level % 2 == 0 else along_second(value)
        store(outgoing, level, k, split, matrix(level, 1 - bit, bit))
        swap(level, k).start()
        store(held, level, k, split, matrix(level, bit, bit))

    def enter(k):
        base_super = lax.rem(k, parts) * SUPERS
        targets = [target_of(z * slots + k // parts) for z in range(narrow)]
        for code in range(codes):
            whole = wide_place * codes + code
            add_across = (2 * (whole >> 1 & 1) + (whole >> 3 & 1)).astype(jnp.float32)
            add_down = (2 * (whole & 1) + (whole >> 2 & 1)).astype(jnp.float32)
            offset_across = nodes_across + add_across
            offset_down = nodes_down + add_down
            across = (offset_across - 2.0) * 0.25
            down = (offset_down - 2.0) * down_scale
            for index in range(SUPERS):
                lengths = radial(k, index, offset_across, offset_down)
                for z, (box, center_across, center_down, speed) in enumerate(targets):
                    cosine, sine = turned(
                        center_across * across + center_down * down + speed * lengths
                    )
                    real = weights_ref[code, base_super + index, box, 0]
                    imag = weights_ref[code, base_super + index, box, 1]
                    held[k, z, code, index, 0] = real * cosine + imag * sine
                    held[k, z, code, index, 1] = imag * cosine - real * sine
        exchange(0, k, held[k])

    def middle(level, k):
        swap(level - 1, k).wait()
        exchange(level, k, held[k] + arrived[level - 1, k])

    def leave(k):
        swap(partner_levels - 1, k).wait()
        value = held[k] + arrived[partner_levels - 1, k]
        results = []
        if partner_levels == 4:
            results.append((value[:, 0, :, 0], value[:, 0, :, 1]))
        else:
            splits = [along_second(value[:, child : child + 1]) for child in range(2)]
            for target in range(2):
                total = second_product(splits[0], matrix(3, target, 0))
                total = total + second_product(splits[1], matrix(3, target, 1))
                shape = (narrow, SUPERS, 8, 128)
                results.append((total[:, :128].reshape(shape), total[:, 128:].reshape(shape)))
        targets = [target_of(z * slots + k // parts) for z in range(narrow)]
        across = nodes_across - 0.5
        down = (4.0 * nodes_down - 2.0) * down_scale
        for index in range(SUPERS):
            lengths = radial(k, index, 4.0 * nodes_across, 4.0 * nodes_down)
            for z, (_, center_across, center_down, speed) in enumerate(targets):
                cosine, sine = turned(
                    center_across * across + center_down * down + speed * lengths
                )
                for code, (real, imag) in enumerate(results):
                    real, imag = real[z, index], imag[z, index]
                    outgoing[k, z, code, index, 0] = real * cosine - imag * sine
                    outgoing[k, z, code, index, 1] = real * sine + imag * cosine
        for step in range(1, narrow):
            hand_over(step, k).start()
        hand_own(k).start()

    stages = [(0, enter)]
    for level in range(1, partner_levels):
        stages.append((2 * level, functools.partial(middle, level)))
    stages.append((2 * partner_levels - 1, leave))

    def turn(now, carry):
        for lag, stage in stages:
            k = now - lag
            pl.when((k >= 0) & (k < chunks))(functools.partial(stage, k))
        return carry

    lax.fori_loop(0, chunks + stages[-1][0], turn, 0)

    def finish(k, carry):
        for step in range(1, narrow):
            hand_over(step, k).wait()
        hand_own(k).wait()
        return carry

    lax.fori_loop(0, chunks, finish, 0)


def local(weights_in, medium_speed, target_order):
    wide = lax.axis_size("wide")
    narrow = lax.axis_size("narrow")
    codes, supers, tiles = weights_in.shape[:3]
    slots = tiles // narrow
    chunks = slots * (supers // SUPERS)
    partner_levels = wide.bit_length() - 1
    nodes = cheb_nodes().astype(np.float32)
    node_table = np.stack(
        [np.repeat(nodes[:, None], 128, axis=1), np.repeat(np.repeat(nodes, 16)[None], 8, axis=0)]
    )
    chunk_shape = (narrow, codes, SUPERS, 2, 8, 128)
    sizes = (wide, narrow, codes, supers, slots)
    scalars = pl.BlockSpec(memory_space=pltpu.SMEM)
    vectors = pl.BlockSpec(memory_space=pltpu.VMEM)
    return pl.pallas_call(
        functools.partial(kernel, sizes),
        out_shape=jax.ShapeDtypeStruct(
            (codes, slots, supers * narrow) + weights_in.shape[3:], jnp.float32
        ),
        in_specs=[scalars, scalars, vectors, vectors, vectors],
        out_specs=pl.BlockSpec(memory_space=pl.ANY),
        scratch_shapes=[
            pltpu.VMEM((chunks,) + chunk_shape, jnp.float32),
            pltpu.VMEM((chunks,) + chunk_shape, jnp.float32),
            pltpu.VMEM((partner_levels, chunks) + chunk_shape, jnp.float32),
            pltpu.SemaphoreType.DMA((partner_levels, chunks)),
            pltpu.SemaphoreType.DMA((partner_levels, chunks)),
            pltpu.SemaphoreType.DMA((narrow - 1, chunks)),
            pltpu.SemaphoreType.DMA((narrow - 1, chunks)),
            pltpu.SemaphoreType.DMA((chunks,)),
        ],
        compiler_params=pltpu.CompilerParams(
            collective_id=0, has_side_effects=True, vmem_limit_bytes=62 * 2**20
        ),
    )(
        target_order,
        medium_speed.reshape(-1),
        weights_in,
        jnp.asarray(all_matrices(8 * narrow)),
        jnp.asarray(node_table),
    )


def solution(mesh):
    in_specs = (P("wide", "narrow", None, None, None, None), P(), P())
    out_specs = P("wide", "narrow", None, None, None, None)
    return jax.shard_map(local, mesh=mesh, in_specs=in_specs, out_specs=out_specs, check_vma=False)
```

```python
import functools

import jax
import jax.numpy as jnp
import ml_dtypes
import numpy as np
from jax import lax
from jax.experimental import pallas as pl
from jax.experimental.pallas import tpu as pltpu
from jax.sharding import PartitionSpec as P

TX = 8
TY = 8
SYH = 4
SUPERS = 4

MESH = pl.DeviceIdType.MESH
REGROUP = -1
level_bits = (3, 2, 1, 0)


def cheb_nodes():
    return 0.5 - 0.5 * np.cos(np.pi * (2.0 * np.arange(8) + 1.0) / 16.0)


def lagrange_matrix(child):
    nodes = cheb_nodes()
    points = (child + nodes) / 2.0
    matrix = np.ones((8, 8))
    for q in range(8):
        for m in range(8):
            if m != q:
                matrix[q] *= (points - nodes[m]) / (nodes[q] - nodes[m])
    return matrix


def level_matrix(level, across_boxes, high, target, child):
    nodes = cheb_nodes()
    merges = 1 + level // 2
    boxes = across_boxes if level % 2 == 0 else 4 * SYH
    tiles = TX if level % 2 == 0 else TY
    side = 2.0**merges / boxes
    if merges == 1:
        shift = (target - 0.5) / (2 * tiles)
    else:
        shift = (2 * high + target - 1.5) / (4 * tiles)
    wave = np.pi * across_boxes / 2.0 * shift * side
    parent = np.exp(1j * wave * (nodes - 0.5))
    inner = np.exp(-1j * wave * ((child + nodes) / 2.0 - 0.5))
    matrix = parent[:, None] * lagrange_matrix(child) * inner[None, :]
    return np.block([[matrix.real, -matrix.imag], [matrix.imag, matrix.real]])


def all_matrices(across_boxes):
    found = []
    for level in range(4):
        for high in range(1 if level < 2 else 2):
            for target in range(2):
                for child in range(2):
                    small = level_matrix(level, across_boxes, high, target, child)
                    if level % 2 == 0:
                        big = np.kron(np.eye(16), small)
                    else:
                        big = np.kron(small.T, np.eye(16))
                    first = big.astype(np.float32).astype(ml_dtypes.bfloat16)
                    rest = (big - first.astype(np.float64)).astype(np.float32)
                    found.append(np.stack([first, rest.astype(ml_dtypes.bfloat16)]))
    return np.stack(found)


def turned(turns):
    part = turns - jnp.floor(turns + 0.5)
    half = part * np.float32(np.pi)
    square = half * half
    sine = np.float32(-1.0 / 39916800.0)
    for value in (1.0 / 362880.0, -1.0 / 5040.0, 1.0 / 120.0, -1.0 / 6.0, 1.0):
        sine = sine * square + np.float32(value)
    sine = sine * half
    cosine = np.float32(1.0 / 479001600.0)
    for value in (-1.0 / 3628800.0, 1.0 / 40320.0, -1.0 / 720.0, 1.0 / 24.0, -0.5, 1.0):
        cosine = cosine * square + np.float32(value)
    return 1.0 - 2.0 * sine * sine, 2.0 * sine * cosine


def late_chunks(chunks):
    return chunks // 3


def split_two(value):
    first = value.astype(jnp.bfloat16)
    return first, (value - first.astype(jnp.float32)).astype(jnp.bfloat16)


def dot(left, right):
    return jnp.dot(left, right, preferred_element_type=jnp.float32)


def kernel(
    sizes,
    order_ref,
    speed_ref,
    weights_in_ref,
    all_mats_ref,
    nodes_ref,
    out_ref,
    weights_ref,
    mats_ref,
    held,
    outgoing,
    arrived,
    grouped,
    weights_sem,
    mats_sem,
    send_sem,
    recv_sem,
    far_send,
    far_recv,
    own_sem,
):
    wide, narrow, codes, supers, slots = sizes
    partner_levels = wide.bit_length() - 1
    local_bits = codes.bit_length() - 1
    parts = supers // SUPERS
    chunks = slots * parts
    across_boxes = 8 * narrow
    boxes = narrow * codes * SUPERS
    first_grouped = late_chunks(chunks)
    wide_place = lax.axis_index("wide")
    narrow_place = lax.axis_index("narrow")

    def device_bit(level):
        return wide_place >> (level_bits[level] - local_bits) & 1

    def partner(level):
        step = 1 << (level_bits[level] - local_bits)
        return wide_place + step * (1 - 2 * device_bit(level))

    copies = [pltpu.make_async_copy(weights_in_ref, weights_ref, weights_sem)]
    wanted = []
    for level in range(partner_levels):
        wanted.append((level, device_bit(level), device_bit(level)))
        wanted.append((level, 1 - device_bit(level), device_bit(level)))
    for level in range(partner_levels, 4):
        wanted.extend((level, target, child) for target in range(2) for child in range(2))
    for place, (level, target, child) in enumerate(wanted):
        if level < 2:
            source = 4 * level + 2 * target + child
        else:
            source = 8 * level - 8 + 4 * device_bit(level - 2) + 2 * target + child
        copies.append(
            pltpu.make_async_copy(all_mats_ref.at[source], mats_ref.at[place], mats_sem.at[place])
        )
    for copy in copies:
        copy.start()

    def matrix(place):
        return mats_ref[place, 0], mats_ref[place, 1]

    def far(step):
        return lax.rem(narrow_place + step, narrow)

    barrier = pltpu.get_barrier_semaphore()
    for level in range(partner_levels):
        pl.semaphore_signal(
            barrier, inc=1, device_id={"wide": partner(level)}, device_id_type=MESH
        )
    for step in range(1, narrow):
        pl.semaphore_signal(barrier, inc=1, device_id={"narrow": far(step)}, device_id_type=MESH)
    pl.semaphore_wait(barrier, partner_levels + narrow - 1)
    for copy in copies:
        copy.wait()

    def swap(level, k):
        return pltpu.make_async_remote_copy(
            src_ref=outgoing.at[k],
            dst_ref=arrived.at[level, k],
            send_sem=send_sem.at[level, k],
            recv_sem=recv_sem.at[level, k],
            device_id={"wide": partner(level)},
            device_id_type=MESH,
        )

    def place_of(k, z):
        return out_ref.at[:, k // parts, pl.ds(z * supers + lax.rem(k, parts) * SUPERS, SUPERS)]

    def hand_over(step, k, late):
        return pltpu.make_async_remote_copy(
            src_ref=outgoing.at[k, far(step)],
            dst_ref=place_of(k, narrow_place) if late else grouped.at[k - first_grouped, narrow_place],
            send_sem=far_send.at[step - 1, k],
            recv_sem=far_recv.at[step - 1, k],
            device_id={"narrow": far(step)},
            device_id_type=MESH,
        )

    def write_out(k, z):
        return pltpu.make_async_copy(outgoing.at[k, z], place_of(k, z), own_sem.at[z, k])

    def target_of(slot):
        box = order_ref[slot]
        speed = speed_ref[box // TY, box % TY]
        center_across = ((box // TY).astype(jnp.float32) + 0.5) * np.float32(1.0 / TX)
        center_down = ((box % TY).astype(jnp.float32) + 0.5) * np.float32(1.0 / TY)
        return box, center_across, center_down, speed * np.float32(across_boxes / 4.0)

    def radial(k, z, index, offset_across, offset_down):
        place = z * supers + lax.rem(k, parts) * SUPERS + index
        corner_across = (4 * (place // SYH)).astype(jnp.float32)
        corner_down = (4 * (place % SYH)).astype(jnp.float32)
        unit_across = np.float32(1.0 / across_boxes)
        unit_down = np.float32(1.0 / (4 * SYH))
        first = (corner_across + offset_across) * unit_across
        second = (corner_down + offset_down) * unit_down
        base_first = jnp.full((8, 128), (corner_across + 2.0) * unit_across)
        base_second = jnp.full((8, 128), (corner_down + 2.0) * unit_down)
        square = first * first + second * second
        base = base_first * base_first + base_second * base_second
        return (square - base) / (jnp.sqrt(square) + jnp.sqrt(base))

    nodes_across = nodes_ref[0]
    nodes_down = nodes_ref[1]
    down_scale = np.float32(across_boxes / 4.0 / (4 * SYH))

    def along_first(value):
        rows = value.reshape(boxes * 16, 128)
        pieces = [rows[256 * n : 256 * n + 256] for n in range(boxes // 16)]
        return split_two(jnp.concatenate(pieces, axis=1))

    def first_product(split, pair):
        total = dot(pair[0], split[0]) + dot(pair[0], split[1]) + dot(pair[1], split[0])
        pieces = [total[:, 128 * n : 128 * n + 128] for n in range(boxes // 16)]
        return jnp.concatenate(pieces, axis=0).reshape(narrow, codes, SUPERS, 2, 8, 128)

    def along_second(value):
        count = value.shape[0] * value.shape[1] * value.shape[2] * 8
        real = value[:, :, :, 0].reshape(count, 128)
        imag = value[:, :, :, 1].reshape(count, 128)
        return split_two(jnp.concatenate([real, imag], axis=1))

    def second_product(split, pair):
        return dot(split[0], pair[0]) + dot(split[1], pair[0]) + dot(split[0], pair[1])

    def store(into, level, k, split, pair):
        if level % 2 == 0:
            into[k] = first_product(split, pair)
        else:
            total = second_product(split, pair)
            shape = (narrow, codes, SUPERS, 8, 128)
            into[k, :, :, :, 0] = total[:, :128].reshape(shape)
            into[k, :, :, :, 1] = total[:, 128:].reshape(shape)

    def exchange(level, k, value):
        split = along_first(value) if level % 2 == 0 else along_second(value)
        store(outgoing, level, k, split, matrix(2 * level + 1))
        swap(level, k).start()
        store(held, level, k, split, matrix(2 * level))

    def regroup(k):
        for step in range(1, narrow):
            hand_over(step, k, False).start()
        grouped[k - first_grouped, narrow_place] = outgoing[k, narrow_place]

    def phased(k, into):
        base_super = lax.rem(k, parts) * SUPERS
        targets = [target_of(z * slots + k // parts) for z in range(narrow)]
        for code in range(codes):
            whole = wide_place * codes + code
            add_across = (2 * (whole >> 1 & 1) + (whole >> 3 & 1)).astype(jnp.float32)
            add_down = (2 * (whole & 1) + (whole >> 2 & 1)).astype(jnp.float32)
            offset_across = nodes_across + add_across
            offset_down = nodes_down + add_down
            across = (offset_across - 2.0) * 0.25
            down = (offset_down - 2.0) * down_scale
            for index in range(SUPERS):
                lengths = radial(k, narrow_place, index, offset_across, offset_down)
                for z, (box, center_across, center_down, speed) in enumerate(targets):
                    cosine, sine = turned(
                        center_across * across + center_down * down + speed * lengths
                    )
                    real = weights_ref[code, base_super + index, box, 0]
                    imag = weights_ref[code, base_super + index, box, 1]
                    into[k, z, code, index, 0] = real * cosine + imag * sine
                    into[k, z, code, index, 1] = imag * cosine - real * sine

    def finished(k, value, late):
        results = []
        if partner_levels == 4:
            results.append((value[:, 0, :, 0], value[:, 0, :, 1]))
        else:
            splits = [along_second(value[:, child : child + 1]) for child in range(2)]
            for target in range(2):
                total = second_product(splits[0], matrix(6 + 2 * target))
                total = total + second_product(splits[1], matrix(7 + 2 * target))
                shape = (narrow, SUPERS, 8, 128)
                results.append((total[:, :128].reshape(shape), total[:, 128:].reshape(shape)))
        across = nodes_across - 0.5
        down = (4.0 * nodes_down - 2.0) * down_scale
        for z in range(narrow):
            slot = (z if late else narrow_place) * slots + k // parts
            _, center_across, center_down, speed = target_of(slot)
            linear = center_across * across + center_down * down
            for index in range(SUPERS):
                source = narrow_place if late else z
                lengths = radial(k, source, index, 4.0 * nodes_across, 4.0 * nodes_down)
                cosine, sine = turned(linear + speed * lengths)
                for code, (real, imag) in enumerate(results):
                    real, imag = real[z, index], imag[z, index]
                    outgoing[k, z, code, index, 0] = real * cosine - imag * sine
                    outgoing[k, z, code, index, 1] = real * sine + imag * cosine

    def stage(steps, place, k):
        late = REGROUP not in steps
        if place == 0:
            if steps[0] == REGROUP:
                phased(k, outgoing)
                regroup(k)
            else:
                phased(k, held)
                exchange(steps[0], k, held[k])
            return
        before = steps[place - 1]
        if before == REGROUP:
            for step in range(1, narrow):
                hand_over(step, k, False).wait()
            value = grouped[k - first_grouped]
        else:
            swap(before, k).wait()
            value = held[k] + arrived[before, k]
        if place == len(steps):
            finished(k, value, late)
            if late:
                for step in range(1, narrow):
                    hand_over(step, k, True).start()
                write_out(k, narrow_place).start()
            else:
                for z in range(narrow):
                    write_out(k, z).start()
        elif steps[place] == REGROUP:
            outgoing[k] = value
            regroup(k)
        else:
            exchange(steps[place], k, value)

    rest = tuple(range(2, partner_levels))
    orders = [((0, 1) + rest, 0, first_grouped)]
    middle = first_grouped + (chunks - first_grouped) // 2
    orders.append(((1, REGROUP, 0) + rest, first_grouped, middle))
    orders.append(((REGROUP, 0, 1) + rest, middle, chunks))
    depth = max(len(steps) for steps, _, _ in orders)
    turns = max(last - first for _, first, last in orders)

    def turn(now, carry):
        for place in range(depth + 1):
            for steps, first, last in orders:
                if place <= len(steps):
                    k = first + now - place
                    pl.when((k >= first) & (k < last))(functools.partial(stage, steps, place, k))
        return carry

    lax.fori_loop(0, turns + depth, turn, 0)

    def finish_late(k, carry):
        for step in range(1, narrow):
            hand_over(step, k, True).wait()
        write_out(k, narrow_place).wait()
        return carry

    def finish(k, carry):
        for z in range(narrow):
            write_out(k, z).wait()
        return carry

    lax.fori_loop(first_grouped, chunks, finish, 0)
    lax.fori_loop(0, first_grouped, finish_late, 0)


def local(weights_in, medium_speed, target_order):
    wide = lax.axis_size("wide")
    narrow = lax.axis_size("narrow")
    codes, supers, tiles = weights_in.shape[:3]
    slots = tiles // narrow
    chunks = slots * (supers // SUPERS)
    partner_levels = wide.bit_length() - 1
    nodes = cheb_nodes().astype(np.float32)
    node_table = np.stack(
        [np.repeat(nodes[:, None], 128, axis=1), np.repeat(np.repeat(nodes, 16)[None], 8, axis=0)]
    )
    chunk_shape = (narrow, codes, SUPERS, 2, 8, 128)
    sizes = (wide, narrow, codes, supers, slots)
    scalars = pl.BlockSpec(memory_space=pltpu.SMEM)
    vectors = pl.BlockSpec(memory_space=pltpu.VMEM)
    anywhere = pl.BlockSpec(memory_space=pl.ANY)
    matrices = 2 * partner_levels + 4 * (4 - partner_levels)
    return pl.pallas_call(
        functools.partial(kernel, sizes),
        out_shape=jax.ShapeDtypeStruct(
            (codes, slots, supers * narrow) + weights_in.shape[3:], jnp.float32
        ),
        in_specs=[scalars, scalars, anywhere, anywhere, vectors],
        out_specs=anywhere,
        scratch_shapes=[
            pltpu.VMEM(weights_in.shape, jnp.float32),
            pltpu.VMEM((matrices, 2, 256, 256), jnp.bfloat16),
            pltpu.VMEM((chunks,) + chunk_shape, jnp.float32),
            pltpu.VMEM((chunks,) + chunk_shape, jnp.float32),
            pltpu.VMEM((partner_levels, chunks) + chunk_shape, jnp.float32),
            pltpu.VMEM((chunks - late_chunks(chunks),) + chunk_shape, jnp.float32),
            pltpu.SemaphoreType.DMA,
            pltpu.SemaphoreType.DMA((matrices,)),
            pltpu.SemaphoreType.DMA((partner_levels, chunks)),
            pltpu.SemaphoreType.DMA((partner_levels, chunks)),
            pltpu.SemaphoreType.DMA((narrow - 1, chunks)),
            pltpu.SemaphoreType.DMA((narrow - 1, chunks)),
            pltpu.SemaphoreType.DMA((narrow, chunks)),
        ],
        compiler_params=pltpu.CompilerParams(
            collective_id=0, has_side_effects=True, vmem_limit_bytes=62 * 2**20
        ),
    )(
        target_order,
        medium_speed,
        weights_in,
        jnp.asarray(all_matrices(8 * narrow)),
        jnp.asarray(node_table),
    )


def solution(mesh):
    in_specs = (P("wide", "narrow", None, None, None, None), P(), P())
    out_specs = P("wide", "narrow", None, None, None, None)
    return jax.shard_map(local, mesh=mesh, in_specs=in_specs, out_specs=out_specs, check_vma=False)
```

```python
import functools

import jax
import jax.numpy as jnp
import ml_dtypes
import numpy as np
from jax import lax
from jax.experimental import pallas as pl
from jax.experimental.pallas import tpu as pltpu
from jax.sharding import PartitionSpec as P

TX = 8
TY = 8
SYH = 4
SUPERS = 4

MESH = pl.DeviceIdType.MESH
REGROUP = -1
level_bits = (3, 2, 1, 0)


def cheb_nodes():
    return 0.5 - 0.5 * np.cos(np.pi * (2.0 * np.arange(8) + 1.0) / 16.0)


def lagrange_matrix(child):
    nodes = cheb_nodes()
    points = (child + nodes) / 2.0
    matrix = np.ones((8, 8))
    for q in range(8):
        for m in range(8):
            if m != q:
                matrix[q] *= (points - nodes[m]) / (nodes[q] - nodes[m])
    return matrix


def level_matrix(level, across_boxes, high, target, child):
    nodes = cheb_nodes()
    merges = 1 + level // 2
    boxes = across_boxes if level % 2 == 0 else 4 * SYH
    tiles = TX if level % 2 == 0 else TY
    side = 2.0**merges / boxes
    if merges == 1:
        shift = (target - 0.5) / (2 * tiles)
    else:
        shift = (2 * high + target - 1.5) / (4 * tiles)
    wave = np.pi * across_boxes / 2.0 * shift * side
    parent = np.exp(1j * wave * (nodes - 0.5))
    inner = np.exp(-1j * wave * ((child + nodes) / 2.0 - 0.5))
    matrix = parent[:, None] * lagrange_matrix(child) * inner[None, :]
    return np.block([[matrix.real, -matrix.imag], [matrix.imag, matrix.real]])


def all_matrices(across_boxes):
    found = []
    for level in range(4):
        for high in range(1 if level < 2 else 2):
            for target in range(2):
                for child in range(2):
                    small = level_matrix(level, across_boxes, high, target, child)
                    if level % 2 == 0:
                        big = np.kron(np.eye(16), small)
                    else:
                        big = np.kron(small.T, np.eye(16))
                    first = big.astype(np.float32).astype(ml_dtypes.bfloat16)
                    rest = (big - first.astype(np.float64)).astype(np.float32)
                    found.append(np.stack([first, rest.astype(ml_dtypes.bfloat16)]))
    return np.stack(found)


def turned(turns):
    part = turns - jnp.floor(turns + 0.5)
    half = part * np.float32(np.pi)
    square = half * half
    sine = np.float32(-1.0 / 39916800.0)
    for value in (1.0 / 362880.0, -1.0 / 5040.0, 1.0 / 120.0, -1.0 / 6.0, 1.0):
        sine = sine * square + np.float32(value)
    sine = sine * half
    cosine = np.float32(1.0 / 479001600.0)
    for value in (-1.0 / 3628800.0, 1.0 / 40320.0, -1.0 / 720.0, 1.0 / 24.0, -0.5, 1.0):
        cosine = cosine * square + np.float32(value)
    return 1.0 - 2.0 * sine * sine, 2.0 * sine * cosine


def late_chunks(chunks):
    return (chunks + 1) // 3


def split_two(value):
    first = value.astype(jnp.bfloat16)
    return first, (value - first.astype(jnp.float32)).astype(jnp.bfloat16)


def dot(left, right):
    return jnp.dot(left, right, preferred_element_type=jnp.float32)


def kernel(
    sizes,
    order_ref,
    speed_ref,
    weights_in_ref,
    all_mats_ref,
    nodes_ref,
    out_ref,
    weights_ref,
    mats_ref,
    held,
    outgoing,
    arrived,
    grouped,
    weights_sem,
    mats_sem,
    send_sem,
    recv_sem,
    far_send,
    far_recv,
    own_sem,
):
    wide, narrow, codes, supers, slots = sizes
    partner_levels = wide.bit_length() - 1
    local_bits = codes.bit_length() - 1
    parts = supers // SUPERS
    chunks = slots * parts
    across_boxes = 8 * narrow
    boxes = narrow * codes * SUPERS
    first_grouped = late_chunks(chunks)
    wide_place = lax.axis_index("wide")
    narrow_place = lax.axis_index("narrow")

    def device_bit(level):
        return wide_place >> (level_bits[level] - local_bits) & 1

    def partner(level):
        step = 1 << (level_bits[level] - local_bits)
        return wide_place + step * (1 - 2 * device_bit(level))

    copies = []
    for code in range(codes):
        for part in range(parts):
            piece = (code, pl.ds(part * SUPERS, SUPERS))
            copies.append(
                pltpu.make_async_copy(
                    weights_in_ref.at[piece], weights_ref.at[piece], weights_sem.at[code, part]
                )
            )
    wanted = []
    for level in range(partner_levels):
        wanted.append((level, device_bit(level), device_bit(level)))
        wanted.append((level, 1 - device_bit(level), device_bit(level)))
    for level in range(partner_levels, 4):
        wanted.extend((level, target, child) for target in range(2) for child in range(2))
    for place, (level, target, child) in enumerate(wanted):
        if level < 2:
            source = 4 * level + 2 * target + child
        else:
            source = 8 * level - 8 + 4 * device_bit(level - 2) + 2 * target + child
        copies.append(
            pltpu.make_async_copy(all_mats_ref.at[source], mats_ref.at[place], mats_sem.at[place])
        )
    for copy in copies:
        copy.start()

    def matrix(place):
        return mats_ref[place, 0], mats_ref[place, 1]

    def far(step):
        return lax.rem(narrow_place + step, narrow)

    barrier = pltpu.get_barrier_semaphore()
    for level in range(partner_levels):
        pl.semaphore_signal(
            barrier, inc=1, device_id={"wide": partner(level)}, device_id_type=MESH
        )
    for step in range(1, narrow):
        pl.semaphore_signal(barrier, inc=1, device_id={"narrow": far(step)}, device_id_type=MESH)
    pl.semaphore_wait(barrier, partner_levels + narrow - 1)
    for copy in copies:
        copy.wait()

    def swap(level, k):
        return pltpu.make_async_remote_copy(
            src_ref=outgoing.at[k],
            dst_ref=arrived.at[level, k],
            send_sem=send_sem.at[level, k],
            recv_sem=recv_sem.at[level, k],
            device_id={"wide": partner(level)},
            device_id_type=MESH,
        )

    def place_of(k, z):
        return out_ref.at[:, k // parts, pl.ds(z * supers + lax.rem(k, parts) * SUPERS, SUPERS)]

    def hand_over(step, k, late):
        return pltpu.make_async_remote_copy(
            src_ref=outgoing.at[k, far(step)],
            dst_ref=place_of(k, narrow_place) if late else grouped.at[k - first_grouped, narrow_place],
            send_sem=far_send.at[step - 1, k],
            recv_sem=far_recv.at[step - 1, k],
            device_id={"narrow": far(step)},
            device_id_type=MESH,
        )

    def write_out(k, z):
        return pltpu.make_async_copy(outgoing.at[k, z], place_of(k, z), own_sem.at[z, k])

    def target_of(slot):
        box = order_ref[slot]
        speed = speed_ref[box // TY, box % TY]
        center_across = ((box // TY).astype(jnp.float32) + 0.5) * np.float32(1.0 / TX)
        center_down = ((box % TY).astype(jnp.float32) + 0.5) * np.float32(1.0 / TY)
        return box, center_across, center_down, speed * np.float32(across_boxes / 4.0)

    def radial(k, z, index, offset_across, offset_down):
        place = z * supers + lax.rem(k, parts) * SUPERS + index
        corner_across = (4 * (place // SYH)).astype(jnp.float32)
        corner_down = (4 * (place % SYH)).astype(jnp.float32)
        unit_across = np.float32(1.0 / across_boxes)
        unit_down = np.float32(1.0 / (4 * SYH))
        first = (corner_across + offset_across) * unit_across
        second = (corner_down + offset_down) * unit_down
        base_first = jnp.full((8, 128), (corner_across + 2.0) * unit_across)
        base_second = jnp.full((8, 128), (corner_down + 2.0) * unit_down)
        square = first * first + second * second
        base = base_first * base_first + base_second * base_second
        return (square - base) / (jnp.sqrt(square) + jnp.sqrt(base))

    nodes_across = nodes_ref[0]
    nodes_down = nodes_ref[1]
    down_scale = np.float32(across_boxes / 4.0 / (4 * SYH))

    def along_first(value):
        rows = value.reshape(boxes * 16, 128)
        pieces = [rows[256 * n : 256 * n + 256] for n in range(boxes // 16)]
        first, rest = split_two(jnp.concatenate(pieces, axis=1))
        return jnp.concatenate([first, rest, first], axis=0)

    def first_product(split, pair):
        total = dot(jnp.concatenate([pair[0], pair[0], pair[1]], axis=1), split)
        pieces = [total[:, 128 * n : 128 * n + 128] for n in range(boxes // 16)]
        return jnp.concatenate(pieces, axis=0).reshape(narrow, codes, SUPERS, 2, 8, 128)

    def along_second(value):
        count = value.shape[0] * value.shape[1] * value.shape[2] * 8
        real = value[:, :, :, 0].reshape(count, 128)
        imag = value[:, :, :, 1].reshape(count, 128)
        first, rest = split_two(jnp.concatenate([real, imag], axis=1))
        return jnp.concatenate([first, rest, first], axis=1)

    def second_product(split, *pairs):
        terms = [term for pair in pairs for term in (pair[0], pair[0], pair[1])]
        return dot(split, jnp.concatenate(terms, axis=0))

    def store(into, level, k, split, pair):
        if level % 2 == 0:
            into[k] = first_product(split, pair)
        else:
            total = second_product(split, pair)
            shape = (narrow, codes, SUPERS, 8, 128)
            into[k, :, :, :, 0] = total[:, :128].reshape(shape)
            into[k, :, :, :, 1] = total[:, 128:].reshape(shape)

    def exchange(level, k, value):
        split = along_first(value) if level % 2 == 0 else along_second(value)
        store(outgoing, level, k, split, matrix(2 * level + 1))
        swap(level, k).start()
        store(held, level, k, split, matrix(2 * level))

    def regroup(k):
        for step in range(1, narrow):
            hand_over(step, k, False).start()
        grouped[k - first_grouped, narrow_place] = outgoing[k, narrow_place]

    def phased(k, into):
        base_super = lax.rem(k, parts) * SUPERS
        targets = [target_of(z * slots + k // parts) for z in range(narrow)]
        for code in range(codes):
            whole = wide_place * codes + code
            add_across = (2 * (whole >> 1 & 1) + (whole >> 3 & 1)).astype(jnp.float32)
            add_down = (2 * (whole & 1) + (whole >> 2 & 1)).astype(jnp.float32)
            offset_across = nodes_across + add_across
            offset_down = nodes_down + add_down
            across = (offset_across - 2.0) * 0.25
            down = (offset_down - 2.0) * down_scale
            for index in range(SUPERS):
                lengths = radial(k, narrow_place, index, offset_across, offset_down)
                for z, (box, center_across, center_down, speed) in enumerate(targets):
                    cosine, sine = turned(
                        center_across * across + center_down * down + speed * lengths
                    )
                    real = weights_ref[code, base_super + index, box, 0]
                    imag = weights_ref[code, base_super + index, box, 1]
                    into[k, z, code, index, 0] = real * cosine + imag * sine
                    into[k, z, code, index, 1] = imag * cosine - real * sine

    def finished(k, value, late):
        results = []
        if partner_levels == 4:
            results.append((value[:, 0, :, 0], value[:, 0, :, 1]))
        else:
            splits = [along_second(value[:, child : child + 1]) for child in range(2)]
            split = jnp.concatenate(splits, axis=1)
            for target in range(2):
                total = second_product(split, matrix(6 + 2 * target), matrix(7 + 2 * target))
                shape = (narrow, SUPERS, 8, 128)
                results.append((total[:, :128].reshape(shape), total[:, 128:].reshape(shape)))
        across = nodes_across - 0.5
        down = (4.0 * nodes_down - 2.0) * down_scale
        for z in range(narrow):
            slot = (z if late else narrow_place) * slots + k // parts
            _, center_across, center_down, speed = target_of(slot)
            linear = center_across * across + center_down * down
            for index in range(SUPERS):
                source = narrow_place if late else z
                lengths = radial(k, source, index, 4.0 * nodes_across, 4.0 * nodes_down)
                cosine, sine = turned(linear + speed * lengths)
                for code, (real, imag) in enumerate(results):
                    real, imag = real[z, index], imag[z, index]
                    outgoing[k, z, code, index, 0] = real * cosine - imag * sine
                    outgoing[k, z, code, index, 1] = real * sine + imag * cosine

    def stage(steps, place, k):
        late = REGROUP not in steps
        if place == 0:
            if steps[0] == REGROUP:
                phased(k, outgoing)
                regroup(k)
            else:
                phased(k, held)
                exchange(steps[0], k, held[k])
            return
        before = steps[place - 1]
        if before == REGROUP:
            for step in range(1, narrow):
                hand_over(step, k, False).wait()
            value = grouped[k - first_grouped]
        else:
            swap(before, k).wait()
            value = held[k] + arrived[before, k]
        if place == len(steps):
            finished(k, value, late)
            if late:
                for step in range(1, narrow):
                    hand_over(step, k, True).start()
                write_out(k, narrow_place).start()
            else:
                for z in range(narrow):
                    write_out(k, z).start()
        elif steps[place] == REGROUP:
            outgoing[k] = value
            regroup(k)
        else:
            exchange(steps[place], k, value)

    rest = tuple(range(3, partner_levels))
    orders = [((0, 2, 1) + rest, 0, first_grouped)]
    middle = first_grouped + chunks // 3
    orders.append(((1, REGROUP, 0, 2) + rest, first_grouped, middle))
    orders.append(((REGROUP, 0, 2, 1) + rest, middle, chunks))
    depth = max(len(steps) for steps, _, _ in orders)
    turns = max(last - first for _, first, last in orders)

    def turn(now, carry):
        for place in range(depth + 1):
            for steps, first, last in orders:
                if place <= len(steps):
                    k = first + now - place
                    pl.when((k >= first) & (k < last))(functools.partial(stage, steps, place, k))
        return carry

    lax.fori_loop(0, turns + depth, turn, 0)

    def finish_late(k, carry):
        for step in range(1, narrow):
            hand_over(step, k, True).wait()
        write_out(k, narrow_place).wait()
        return carry

    def finish(k, carry):
        for z in range(narrow):
            write_out(k, z).wait()
        return carry

    lax.fori_loop(first_grouped, chunks, finish, 0)
    lax.fori_loop(0, first_grouped, finish_late, 0)


def local(weights_in, medium_speed, target_order):
    wide = lax.axis_size("wide")
    narrow = lax.axis_size("narrow")
    codes, supers, tiles = weights_in.shape[:3]
    slots = tiles // narrow
    chunks = slots * (supers // SUPERS)
    partner_levels = wide.bit_length() - 1
    nodes = cheb_nodes().astype(np.float32)
    node_table = np.stack(
        [np.repeat(nodes[:, None], 128, axis=1), np.repeat(np.repeat(nodes, 16)[None], 8, axis=0)]
    )
    chunk_shape = (narrow, codes, SUPERS, 2, 8, 128)
    sizes = (wide, narrow, codes, supers, slots)
    scalars = pl.BlockSpec(memory_space=pltpu.SMEM)
    vectors = pl.BlockSpec(memory_space=pltpu.VMEM)
    anywhere = pl.BlockSpec(memory_space=pl.ANY)
    matrices = 2 * partner_levels + 4 * (4 - partner_levels)
    return pl.pallas_call(
        functools.partial(kernel, sizes),
        out_shape=jax.ShapeDtypeStruct(
            (codes, slots, supers * narrow) + weights_in.shape[3:], jnp.float32
        ),
        in_specs=[scalars, scalars, anywhere, anywhere, vectors],
        out_specs=anywhere,
        scratch_shapes=[
            pltpu.VMEM(weights_in.shape, jnp.float32),
            pltpu.VMEM((matrices, 2, 256, 256), jnp.bfloat16),
            pltpu.VMEM((chunks,) + chunk_shape, jnp.float32),
            pltpu.VMEM((chunks,) + chunk_shape, jnp.float32),
            pltpu.VMEM((partner_levels, chunks) + chunk_shape, jnp.float32),
            pltpu.VMEM((chunks - late_chunks(chunks),) + chunk_shape, jnp.float32),
            pltpu.SemaphoreType.DMA((codes, supers // SUPERS)),
            pltpu.SemaphoreType.DMA((matrices,)),
            pltpu.SemaphoreType.DMA((partner_levels, chunks)),
            pltpu.SemaphoreType.DMA((partner_levels, chunks)),
            pltpu.SemaphoreType.DMA((narrow - 1, chunks)),
            pltpu.SemaphoreType.DMA((narrow - 1, chunks)),
            pltpu.SemaphoreType.DMA((narrow, chunks)),
        ],
        compiler_params=pltpu.CompilerParams(
            collective_id=0, has_side_effects=True, vmem_limit_bytes=62 * 2**20
        ),
    )(
        target_order,
        medium_speed,
        weights_in,
        jnp.asarray(all_matrices(8 * narrow)),
        jnp.asarray(node_table),
    )


def solution(mesh):
    in_specs = (P("wide", "narrow", None, None, None, None), P(), P())
    out_specs = P("wide", "narrow", None, None, None, None)
    return jax.shard_map(local, mesh=mesh, in_specs=in_specs, out_specs=out_specs, check_vma=False)
```

```python
import functools

import jax
import jax.numpy as jnp
import ml_dtypes
import numpy as np
from jax import lax
from jax.experimental import pallas as pl
from jax.experimental.pallas import tpu as pltpu
from jax.sharding import PartitionSpec as P

TX = 8
TY = 8
SYH = 4
SUPERS = 4

MESH = pl.DeviceIdType.MESH
REGROUP = -1
level_bits = (3, 2, 1, 0)


def cheb_nodes():
    return 0.5 - 0.5 * np.cos(np.pi * (2.0 * np.arange(8) + 1.0) / 16.0)


def lagrange_matrix(child):
    nodes = cheb_nodes()
    points = (child + nodes) / 2.0
    matrix = np.ones((8, 8))
    for q in range(8):
        for m in range(8):
            if m != q:
                matrix[q] *= (points - nodes[m]) / (nodes[q] - nodes[m])
    return matrix


def level_matrix(level, across_boxes, high, target, child):
    nodes = cheb_nodes()
    merges = 1 + level // 2
    boxes = across_boxes if level % 2 == 0 else 4 * SYH
    tiles = TX if level % 2 == 0 else TY
    side = 2.0**merges / boxes
    if merges == 1:
        shift = (target - 0.5) / (2 * tiles)
    else:
        shift = (2 * high + target - 1.5) / (4 * tiles)
    wave = np.pi * across_boxes / 2.0 * shift * side
    parent = np.exp(1j * wave * (nodes - 0.5))
    inner = np.exp(-1j * wave * ((child + nodes) / 2.0 - 0.5))
    matrix = parent[:, None] * lagrange_matrix(child) * inner[None, :]
    return np.block([[matrix.real, -matrix.imag], [matrix.imag, matrix.real]])


def all_matrices(across_boxes):
    found = []
    for level in range(4):
        for high in range(1 if level < 2 else 2):
            for target in range(2):
                for child in range(2):
                    small = level_matrix(level, across_boxes, high, target, child)
                    if level % 2 == 0:
                        big = np.kron(np.eye(16), small)
                    else:
                        big = np.kron(small.T, np.eye(16))
                    first = big.astype(np.float32).astype(ml_dtypes.bfloat16)
                    rest = (big - first.astype(np.float64)).astype(np.float32)
                    found.append(np.stack([first, rest.astype(ml_dtypes.bfloat16)]))
    return np.stack(found)


def turned(turns):
    part = turns - jnp.floor(turns + 0.5)
    half = part * np.float32(np.pi)
    square = half * half
    sine = np.float32(-1.0 / 39916800.0)
    for value in (1.0 / 362880.0, -1.0 / 5040.0, 1.0 / 120.0, -1.0 / 6.0, 1.0):
        sine = sine * square + np.float32(value)
    sine = sine * half
    cosine = np.float32(1.0 / 479001600.0)
    for value in (-1.0 / 3628800.0, 1.0 / 40320.0, -1.0 / 720.0, 1.0 / 24.0, -0.5, 1.0):
        cosine = cosine * square + np.float32(value)
    return 1.0 - 2.0 * sine * sine, 2.0 * sine * cosine


def late_chunks(chunks):
    return (chunks + 1) // 3


def split_two(value):
    first = value.astype(jnp.bfloat16)
    return first, (value - first.astype(jnp.float32)).astype(jnp.bfloat16)


def dot(left, right):
    return jnp.dot(left, right, preferred_element_type=jnp.float32)


def kernel(
    sizes,
    order_ref,
    speed_ref,
    weights_in_ref,
    all_mats_ref,
    nodes_ref,
    out_ref,
    weights_ref,
    mats_ref,
    held,
    outgoing,
    arrived,
    grouped,
    weights_sem,
    mats_sem,
    send_sem,
    recv_sem,
    far_send,
    far_recv,
    own_sem,
):
    wide, narrow, codes, supers, slots = sizes
    partner_levels = wide.bit_length() - 1
    local_bits = codes.bit_length() - 1
    parts = supers // SUPERS
    chunks = slots * parts
    across_boxes = 8 * narrow
    boxes = narrow * codes * SUPERS
    first_grouped = late_chunks(chunks)
    wide_place = lax.axis_index("wide")
    narrow_place = lax.axis_index("narrow")

    def device_bit(level):
        return wide_place >> (level_bits[level] - local_bits) & 1

    def partner(level):
        step = 1 << (level_bits[level] - local_bits)
        return wide_place + step * (1 - 2 * device_bit(level))

    copies = []
    for code in range(codes):
        for part in range(parts):
            piece = (code, pl.ds(part * SUPERS, SUPERS))
            copies.append(
                pltpu.make_async_copy(
                    weights_in_ref.at[piece], weights_ref.at[piece], weights_sem.at[code, part]
                )
            )
    wanted = []
    for level in range(partner_levels):
        wanted.append((level, device_bit(level), device_bit(level)))
        wanted.append((level, 1 - device_bit(level), device_bit(level)))
    for level in range(partner_levels, 4):
        wanted.extend((level, target, child) for target in range(2) for child in range(2))
    for place, (level, target, child) in enumerate(wanted):
        if level < 2:
            source = 4 * level + 2 * target + child
        else:
            source = 8 * level - 8 + 4 * device_bit(level - 2) + 2 * target + child
        copies.append(
            pltpu.make_async_copy(all_mats_ref.at[source], mats_ref.at[place], mats_sem.at[place])
        )
    for copy in copies:
        copy.start()

    def matrix(place):
        return mats_ref[place, 0], mats_ref[place, 1]

    def far(step):
        return lax.rem(narrow_place + step, narrow)

    barrier = pltpu.get_barrier_semaphore()
    for level in range(partner_levels):
        pl.semaphore_signal(
            barrier, inc=1, device_id={"wide": partner(level)}, device_id_type=MESH
        )
    for step in range(1, narrow):
        pl.semaphore_signal(barrier, inc=1, device_id={"narrow": far(step)}, device_id_type=MESH)
    pl.semaphore_wait(barrier, partner_levels + narrow - 1)
    for copy in copies:
        copy.wait()

    def swap(level, k):
        return pltpu.make_async_remote_copy(
            src_ref=outgoing.at[k],
            dst_ref=arrived.at[level, k],
            send_sem=send_sem.at[level, k],
            recv_sem=recv_sem.at[level, k],
            device_id={"wide": partner(level)},
            device_id_type=MESH,
        )

    def place_of(k, z):
        return out_ref.at[:, k // parts, pl.ds(z * supers + lax.rem(k, parts) * SUPERS, SUPERS)]

    def hand_over(step, k, late):
        return pltpu.make_async_remote_copy(
            src_ref=outgoing.at[k, far(step)],
            dst_ref=place_of(k, narrow_place) if late else grouped.at[k - first_grouped, narrow_place],
            send_sem=far_send.at[step - 1, k],
            recv_sem=far_recv.at[step - 1, k],
            device_id={"narrow": far(step)},
            device_id_type=MESH,
        )

    def write_out(k, z):
        return pltpu.make_async_copy(outgoing.at[k, z], place_of(k, z), own_sem.at[z, k])

    def target_of(slot):
        box = order_ref[slot]
        speed = speed_ref[box // TY, box % TY]
        center_across = ((box // TY).astype(jnp.float32) + 0.5) * np.float32(1.0 / TX)
        center_down = ((box % TY).astype(jnp.float32) + 0.5) * np.float32(1.0 / TY)
        return box, center_across, center_down, speed * np.float32(across_boxes / 4.0)

    def radial(k, z, index, offset_across, offset_down):
        place = z * supers + lax.rem(k, parts) * SUPERS + index
        corner_across = (4 * (place // SYH)).astype(jnp.float32)
        corner_down = (4 * (place % SYH)).astype(jnp.float32)
        unit_across = np.float32(1.0 / across_boxes)
        unit_down = np.float32(1.0 / (4 * SYH))
        first = (corner_across + offset_across) * unit_across
        second = (corner_down + offset_down) * unit_down
        base_first = jnp.full((8, 128), (corner_across + 2.0) * unit_across)
        base_second = jnp.full((8, 128), (corner_down + 2.0) * unit_down)
        square = first * first + second * second
        base = base_first * base_first + base_second * base_second
        return (square - base) / (jnp.sqrt(square) + jnp.sqrt(base))

    nodes_across = nodes_ref[0]
    nodes_down = nodes_ref[1]
    down_scale = np.float32(across_boxes / 4.0 / (4 * SYH))

    def along_first(value):
        rows = value.reshape(boxes * 16, 128)
        pieces = [rows[256 * n : 256 * n + 256] for n in range(boxes // 16)]
        return split_two(jnp.concatenate(pieces, axis=1))

    def first_product(split, pair):
        total = dot(pair[0], split[0]) + dot(pair[0], split[1]) + dot(pair[1], split[0])
        pieces = [total[:, 128 * n : 128 * n + 128] for n in range(boxes // 16)]
        return jnp.concatenate(pieces, axis=0).reshape(narrow, codes, SUPERS, 2, 8, 128)

    def along_second(value):
        count = value.shape[0] * value.shape[1] * value.shape[2] * 8
        real = value[:, :, :, 0].reshape(count, 128)
        imag = value[:, :, :, 1].reshape(count, 128)
        return split_two(jnp.concatenate([real, imag], axis=1))

    def second_product(split, pair):
        return dot(split[0], pair[0]) + dot(split[1], pair[0]) + dot(split[0], pair[1])

    def store(into, level, k, split, pair):
        if level % 2 == 0:
            into[k] = first_product(split, pair)
        else:
            total = second_product(split, pair)
            shape = (narrow, codes, SUPERS, 8, 128)
            into[k, :, :, :, 0] = total[:, :128].reshape(shape)
            into[k, :, :, :, 1] = total[:, 128:].reshape(shape)

    def exchange(level, k, value):
        split = along_first(value) if level % 2 == 0 else along_second(value)
        store(outgoing, level, k, split, matrix(2 * level + 1))
        swap(level, k).start()
        store(held, level, k, split, matrix(2 * level))

    def regroup(k):
        for step in range(1, narrow):
            hand_over(step, k, False).start()
        grouped[k - first_grouped, narrow_place] = outgoing[k, narrow_place]

    def phased(k, into):
        base_super = lax.rem(k, parts) * SUPERS
        targets = [target_of(z * slots + k // parts) for z in range(narrow)]
        for code in range(codes):
            whole = wide_place * codes + code
            add_across = (2 * (whole >> 1 & 1) + (whole >> 3 & 1)).astype(jnp.float32)
            add_down = (2 * (whole & 1) + (whole >> 2 & 1)).astype(jnp.float32)
            offset_across = nodes_across + add_across
            offset_down = nodes_down + add_down
            across = (offset_across - 2.0) * 0.25
            down = (offset_down - 2.0) * down_scale
            for index in range(SUPERS):
                lengths = radial(k, narrow_place, index, offset_across, offset_down)
                for z, (box, center_across, center_down, speed) in enumerate(targets):
                    cosine, sine = turned(
                        center_across * across + center_down * down + speed * lengths
                    )
                    real = weights_ref[code, base_super + index, box, 0]
                    imag = weights_ref[code, base_super + index, box, 1]
                    into[k, z, code, index, 0] = real * cosine + imag * sine
                    into[k, z, code, index, 1] = imag * cosine - real * sine

    def finished(k, value, late):
        results = []
        if partner_levels == 4:
            results.append((value[:, 0, :, 0], value[:, 0, :, 1]))
        else:
            splits = [along_second(value[:, child : child + 1]) for child in range(2)]
            for target in range(2):
                total = second_product(splits[0], matrix(6 + 2 * target))
                total = total + second_product(splits[1], matrix(7 + 2 * target))
                shape = (narrow, SUPERS, 8, 128)
                results.append((total[:, :128].reshape(shape), total[:, 128:].reshape(shape)))
        across = nodes_across - 0.5
        down = (4.0 * nodes_down - 2.0) * down_scale
        for z in range(narrow):
            slot = (z if late else narrow_place) * slots + k // parts
            _, center_across, center_down, speed = target_of(slot)
            linear = center_across * across + center_down * down
            for index in range(SUPERS):
                source = narrow_place if late else z
                lengths = radial(k, source, index, 4.0 * nodes_across, 4.0 * nodes_down)
                cosine, sine = turned(linear + speed * lengths)
                for code, (real, imag) in enumerate(results):
                    real, imag = real[z, index], imag[z, index]
                    outgoing[k, z, code, index, 0] = real * cosine - imag * sine
                    outgoing[k, z, code, index, 1] = real * sine + imag * cosine

    def stage(steps, place, k):
        late = REGROUP not in steps
        if place == 0:
            if steps[0] == REGROUP:
                phased(k, outgoing)
                regroup(k)
            else:
                phased(k, held)
                exchange(steps[0], k, held[k])
            return
        before = steps[place - 1]
        if before == REGROUP:
            for step in range(1, narrow):
                hand_over(step, k, False).wait()
            value = grouped[k - first_grouped]
        else:
            swap(before, k).wait()
            value = held[k] + arrived[before, k]
        if place == len(steps):
            finished(k, value, late)
            if late:
                for step in range(1, narrow):
                    hand_over(step, k, True).start()
                write_out(k, narrow_place).start()
            else:
                for z in range(narrow):
                    write_out(k, z).start()
        elif steps[place] == REGROUP:
            outgoing[k] = value
            regroup(k)
        else:
            exchange(steps[place], k, value)

    rest = tuple(range(3, partner_levels))
    orders = [((0, 2, 1) + rest, 0, first_grouped)]
    middle = first_grouped + chunks // 3
    orders.append(((1, REGROUP, 0, 2) + rest, first_grouped, middle))
    orders.append(((REGROUP, 0, 2, 1) + rest, middle, chunks))
    depth = max(len(steps) for steps, _, _ in orders)
    turns = max(last - first for _, first, last in orders)

    def turn(now, carry):
        for place in range(depth + 1):
            for steps, first, last in orders:
                if place <= len(steps):
                    k = first + now - place
                    pl.when((k >= first) & (k < last))(functools.partial(stage, steps, place, k))
        return carry

    lax.fori_loop(0, turns + depth, turn, 0)

    def finish_late(k, carry):
        for step in range(1, narrow):
            hand_over(step, k, True).wait()
        write_out(k, narrow_place).wait()
        return carry

    def finish(k, carry):
        for z in range(narrow):
            write_out(k, z).wait()
        return carry

    lax.fori_loop(first_grouped, chunks, finish, 0)
    lax.fori_loop(0, first_grouped, finish_late, 0)


def local(weights_in, medium_speed, target_order):
    wide = lax.axis_size("wide")
    narrow = lax.axis_size("narrow")
    codes, supers, tiles = weights_in.shape[:3]
    slots = tiles // narrow
    chunks = slots * (supers // SUPERS)
    partner_levels = wide.bit_length() - 1
    nodes = cheb_nodes().astype(np.float32)
    node_table = np.stack(
        [np.repeat(nodes[:, None], 128, axis=1), np.repeat(np.repeat(nodes, 16)[None], 8, axis=0)]
    )
    chunk_shape = (narrow, codes, SUPERS, 2, 8, 128)
    sizes = (wide, narrow, codes, supers, slots)
    scalars = pl.BlockSpec(memory_space=pltpu.SMEM)
    vectors = pl.BlockSpec(memory_space=pltpu.VMEM)
    anywhere = pl.BlockSpec(memory_space=pl.ANY)
    matrices = 2 * partner_levels + 4 * (4 - partner_levels)
    return pl.pallas_call(
        functools.partial(kernel, sizes),
        out_shape=jax.ShapeDtypeStruct(
            (codes, slots, supers * narrow) + weights_in.shape[3:], jnp.float32
        ),
        in_specs=[scalars, scalars, anywhere, anywhere, vectors],
        out_specs=anywhere,
        scratch_shapes=[
            pltpu.VMEM(weights_in.shape, jnp.float32),
            pltpu.VMEM((matrices, 2, 256, 256), jnp.bfloat16),
            pltpu.VMEM((chunks,) + chunk_shape, jnp.float32),
            pltpu.VMEM((chunks,) + chunk_shape, jnp.float32),
            pltpu.VMEM((partner_levels, chunks) + chunk_shape, jnp.float32),
            pltpu.VMEM((chunks - late_chunks(chunks),) + chunk_shape, jnp.float32),
            pltpu.SemaphoreType.DMA((codes, supers // SUPERS)),
            pltpu.SemaphoreType.DMA((matrices,)),
            pltpu.SemaphoreType.DMA((partner_levels, chunks)),
            pltpu.SemaphoreType.DMA((partner_levels, chunks)),
            pltpu.SemaphoreType.DMA((narrow - 1, chunks)),
            pltpu.SemaphoreType.DMA((narrow - 1, chunks)),
            pltpu.SemaphoreType.DMA((narrow, chunks)),
        ],
        compiler_params=pltpu.CompilerParams(
            collective_id=0, has_side_effects=True, vmem_limit_bytes=62 * 2**20
        ),
    )(
        target_order,
        medium_speed,
        weights_in,
        jnp.asarray(all_matrices(8 * narrow)),
        jnp.asarray(node_table),
    )


def solution(mesh):
    in_specs = (P("wide", "narrow", None, None, None, None), P(), P())
    out_specs = P("wide", "narrow", None, None, None, None)
    return jax.shard_map(local, mesh=mesh, in_specs=in_specs, out_specs=out_specs, check_vma=False)
```

```python
import functools

import jax
import jax.numpy as jnp
import ml_dtypes
import numpy as np
from jax import lax
from jax.experimental import pallas as pl
from jax.experimental.pallas import tpu as pltpu
from jax.sharding import PartitionSpec as P

TX = 8
TY = 8
SYH = 4
SUPERS = 4

MESH = pl.DeviceIdType.MESH
REGROUP = -1
level_bits = (3, 2, 1, 0)


def cheb_nodes():
    return 0.5 - 0.5 * np.cos(np.pi * (2.0 * np.arange(8) + 1.0) / 16.0)


def lagrange_matrix(child):
    nodes = cheb_nodes()
    points = (child + nodes) / 2.0
    matrix = np.ones((8, 8))
    for q in range(8):
        for m in range(8):
            if m != q:
                matrix[q] *= (points - nodes[m]) / (nodes[q] - nodes[m])
    return matrix


def level_matrix(level, across_boxes, high, target, child):
    nodes = cheb_nodes()
    merges = 1 + level // 2
    boxes = across_boxes if level % 2 == 0 else 4 * SYH
    tiles = TX if level % 2 == 0 else TY
    side = 2.0**merges / boxes
    if merges == 1:
        shift = (target - 0.5) / (2 * tiles)
    else:
        shift = (2 * high + target - 1.5) / (4 * tiles)
    wave = np.pi * across_boxes / 2.0 * shift * side
    parent = np.exp(1j * wave * (nodes - 0.5))
    inner = np.exp(-1j * wave * ((child + nodes) / 2.0 - 0.5))
    matrix = parent[:, None] * lagrange_matrix(child) * inner[None, :]
    return np.block([[matrix.real, -matrix.imag], [matrix.imag, matrix.real]])


def all_matrices(across_boxes):
    found = []
    for level in range(4):
        for high in range(1 if level < 2 else 2):
            for target in range(2):
                for child in range(2):
                    small = level_matrix(level, across_boxes, high, target, child)
                    if level % 2 == 0:
                        big = np.kron(np.eye(16), small)
                    else:
                        big = np.kron(small.T, np.eye(16))
                    first = big.astype(np.float32).astype(ml_dtypes.bfloat16)
                    rest = (big - first.astype(np.float64)).astype(np.float32)
                    found.append(np.stack([first, rest.astype(ml_dtypes.bfloat16)]))
    return np.stack(found)


def turned(turns):
    part = turns - jnp.floor(turns + 0.5)
    half = part * np.float32(np.pi)
    square = half * half
    sine = np.float32(-1.0 / 39916800.0)
    for value in (1.0 / 362880.0, -1.0 / 5040.0, 1.0 / 120.0, -1.0 / 6.0, 1.0):
        sine = sine * square + np.float32(value)
    sine = sine * half
    cosine = np.float32(1.0 / 479001600.0)
    for value in (-1.0 / 3628800.0, 1.0 / 40320.0, -1.0 / 720.0, 1.0 / 24.0, -0.5, 1.0):
        cosine = cosine * square + np.float32(value)
    return 1.0 - 2.0 * sine * sine, 2.0 * sine * cosine


def late_chunks(chunks):
    return (chunks + 1) // 3


def split_two(value):
    first = value.astype(jnp.bfloat16)
    return first, (value - first.astype(jnp.float32)).astype(jnp.bfloat16)


def dot(left, right):
    return jnp.dot(left, right, preferred_element_type=jnp.float32)


def kernel(
    sizes,
    order_ref,
    speed_ref,
    weights_in_ref,
    all_mats_ref,
    nodes_ref,
    out_ref,
    weights_ref,
    mats_ref,
    held,
    outgoing,
    arrived,
    grouped,
    weights_sem,
    mats_sem,
    send_sem,
    recv_sem,
    far_send,
    far_recv,
    own_sem,
):
    wide, narrow, codes, supers, slots = sizes
    partner_levels = wide.bit_length() - 1
    local_bits = codes.bit_length() - 1
    parts = supers // SUPERS
    chunks = slots * parts
    across_boxes = 8 * narrow
    boxes = narrow * codes * SUPERS
    first_grouped = late_chunks(chunks)
    wide_place = lax.axis_index("wide")
    narrow_place = lax.axis_index("narrow")

    def device_bit(level):
        return wide_place >> (level_bits[level] - local_bits) & 1

    def partner(level):
        step = 1 << (level_bits[level] - local_bits)
        return wide_place + step * (1 - 2 * device_bit(level))

    copies = []
    for code in range(codes):
        for part in range(parts):
            piece = (code, pl.ds(part * SUPERS, SUPERS))
            copies.append(
                pltpu.make_async_copy(
                    weights_in_ref.at[piece], weights_ref.at[piece], weights_sem.at[code, part]
                )
            )
    wanted = []
    for level in range(partner_levels):
        wanted.append((level, device_bit(level), device_bit(level)))
        wanted.append((level, 1 - device_bit(level), device_bit(level)))
    for level in range(partner_levels, 4):
        wanted.extend((level, target, child) for target in range(2) for child in range(2))
    for place, (level, target, child) in enumerate(wanted):
        if level < 2:
            source = 4 * level + 2 * target + child
        else:
            source = 8 * level - 8 + 4 * device_bit(level - 2) + 2 * target + child
        copies.append(
            pltpu.make_async_copy(all_mats_ref.at[source], mats_ref.at[place], mats_sem.at[place])
        )
    for copy in copies:
        copy.start()

    def matrix(place):
        return mats_ref[place, 0], mats_ref[place, 1]

    def far(step):
        return lax.rem(narrow_place + step, narrow)

    barrier = pltpu.get_barrier_semaphore()
    for level in range(partner_levels):
        pl.semaphore_signal(
            barrier, inc=1, device_id={"wide": partner(level)}, device_id_type=MESH
        )
    for step in range(1, narrow):
        pl.semaphore_signal(barrier, inc=1, device_id={"narrow": far(step)}, device_id_type=MESH)
    pl.semaphore_wait(barrier, partner_levels + narrow - 1)
    for copy in copies:
        copy.wait()

    def swap(level, k):
        return pltpu.make_async_remote_copy(
            src_ref=outgoing.at[k],
            dst_ref=arrived.at[level, k],
            send_sem=send_sem.at[level, k],
            recv_sem=recv_sem.at[level, k],
            device_id={"wide": partner(level)},
            device_id_type=MESH,
        )

    def place_of(k, z):
        return out_ref.at[:, k // parts, pl.ds(z * supers + lax.rem(k, parts) * SUPERS, SUPERS)]

    def hand_over(step, k, late):
        return pltpu.make_async_remote_copy(
            src_ref=outgoing.at[k, far(step)],
            dst_ref=place_of(k, narrow_place) if late else grouped.at[k - first_grouped, narrow_place],
            send_sem=far_send.at[step - 1, k],
            recv_sem=far_recv.at[step - 1, k],
            device_id={"narrow": far(step)},
            device_id_type=MESH,
        )

    def write_out(k, z):
        return pltpu.make_async_copy(outgoing.at[k, z], place_of(k, z), own_sem.at[z, k])

    def target_of(slot):
        box = order_ref[slot]
        speed = speed_ref[box // TY, box % TY]
        center_across = ((box // TY).astype(jnp.float32) + 0.5) * np.float32(1.0 / TX)
        center_down = ((box % TY).astype(jnp.float32) + 0.5) * np.float32(1.0 / TY)
        return box, center_across, center_down, speed * np.float32(across_boxes / 4.0)

    def radial(k, z, index, offset_across, offset_down):
        place = z * supers + lax.rem(k, parts) * SUPERS + index
        corner_across = (4 * (place // SYH)).astype(jnp.float32)
        corner_down = (4 * (place % SYH)).astype(jnp.float32)
        unit_across = np.float32(1.0 / across_boxes)
        unit_down = np.float32(1.0 / (4 * SYH))
        first = (corner_across + offset_across) * unit_across
        second = (corner_down + offset_down) * unit_down
        base_first = jnp.full((8, 128), (corner_across + 2.0) * unit_across)
        base_second = jnp.full((8, 128), (corner_down + 2.0) * unit_down)
        square = first * first + second * second
        base = base_first * base_first + base_second * base_second
        return (square - base) / (jnp.sqrt(square) + jnp.sqrt(base))

    nodes_across = nodes_ref[0]
    nodes_down = nodes_ref[1]
    down_scale = np.float32(across_boxes / 4.0 / (4 * SYH))

    def along_first(value):
        rows = value.reshape(boxes * 16, 128)
        pieces = [rows[256 * n : 256 * n + 256] for n in range(boxes // 16)]
        return split_two(jnp.concatenate(pieces, axis=1))

    def first_product(split, pair):
        total = dot(pair[0], split[0]) + dot(pair[0], split[1]) + dot(pair[1], split[0])
        pieces = [total[:, 128 * n : 128 * n + 128] for n in range(boxes // 16)]
        return jnp.concatenate(pieces, axis=0).reshape(narrow, codes, SUPERS, 2, 8, 128)

    def along_second(value):
        count = value.shape[0] * value.shape[1] * value.shape[2] * 8
        real = value[:, :, :, 0].reshape(count, 128)
        imag = value[:, :, :, 1].reshape(count, 128)
        return split_two(jnp.concatenate([real, imag], axis=1))

    def second_product(split, pair):
        return dot(split[0], pair[0]) + dot(split[1], pair[0]) + dot(split[0], pair[1])

    def store(into, level, k, split, pair):
        if level % 2 == 0:
            into[k] = first_product(split, pair)
        else:
            total = second_product(split, pair)
            shape = (narrow, codes, SUPERS, 8, 128)
            into[k, :, :, :, 0] = total[:, :128].reshape(shape)
            into[k, :, :, :, 1] = total[:, 128:].reshape(shape)

    def exchange(level, k, value):
        split = along_first(value) if level % 2 == 0 else along_second(value)
        store(outgoing, level, k, split, matrix(2 * level + 1))
        swap(level, k).start()
        store(held, level, k, split, matrix(2 * level))

    def regroup(k):
        for step in range(1, narrow):
            hand_over(step, k, False).start()
        grouped[k - first_grouped, narrow_place] = outgoing[k, narrow_place]

    def phased(k, into):
        base_super = lax.rem(k, parts) * SUPERS
        targets = [target_of(z * slots + k // parts) for z in range(narrow)]
        for code in range(codes):
            whole = wide_place * codes + code
            add_across = (2 * (whole >> 1 & 1) + (whole >> 3 & 1)).astype(jnp.float32)
            add_down = (2 * (whole & 1) + (whole >> 2 & 1)).astype(jnp.float32)
            offset_across = nodes_across + add_across
            offset_down = nodes_down + add_down
            across = (offset_across - 2.0) * 0.25
            down = (offset_down - 2.0) * down_scale
            for index in range(SUPERS):
                lengths = radial(k, narrow_place, index, offset_across, offset_down)
                for z, (box, center_across, center_down, speed) in enumerate(targets):
                    cosine, sine = turned(
                        center_across * across + center_down * down + speed * lengths
                    )
                    real = weights_ref[code, base_super + index, box, 0]
                    imag = weights_ref[code, base_super + index, box, 1]
                    into[k, z, code, index, 0] = real * cosine + imag * sine
                    into[k, z, code, index, 1] = imag * cosine - real * sine

    def finished(k, value, late):
        results = []
        if partner_levels == 4:
            results.append((value[:, 0, :, 0], value[:, 0, :, 1]))
        else:
            splits = [along_second(value[:, child : child + 1]) for child in range(2)]
            for target in range(2):
                total = second_product(splits[0], matrix(6 + 2 * target))
                total = total + second_product(splits[1], matrix(7 + 2 * target))
                shape = (narrow, SUPERS, 8, 128)
                results.append((total[:, :128].reshape(shape), total[:, 128:].reshape(shape)))
        across = nodes_across - 0.5
        down = (4.0 * nodes_down - 2.0) * down_scale
        for z in range(narrow):
            slot = (z if late else narrow_place) * slots + k // parts
            _, center_across, center_down, speed = target_of(slot)
            linear = center_across * across + center_down * down
            for index in range(SUPERS):
                source = narrow_place if late else z
                lengths = radial(k, source, index, 4.0 * nodes_across, 4.0 * nodes_down)
                cosine, sine = turned(linear + speed * lengths)
                for code, (real, imag) in enumerate(results):
                    real, imag = real[z, index], imag[z, index]
                    outgoing[k, z, code, index, 0] = real * cosine - imag * sine
                    outgoing[k, z, code, index, 1] = real * sine + imag * cosine

    def stage(steps, place, k):
        late = REGROUP not in steps
        if place == 0:
            if steps[0] == REGROUP:
                phased(k, outgoing)
                regroup(k)
            else:
                phased(k, held)
                exchange(steps[0], k, held[k])
            return
        before = steps[place - 1]
        if before == REGROUP:
            for step in range(1, narrow):
                hand_over(step, k, False).wait()
            value = grouped[k - first_grouped]
        else:
            swap(before, k).wait()
            value = held[k] + arrived[before, k]
        if place == len(steps):
            finished(k, value, late)
            if late:
                for step in range(1, narrow):
                    hand_over(step, k, True).start()
                write_out(k, narrow_place).start()
            else:
                for z in range(narrow):
                    write_out(k, z).start()
        elif steps[place] == REGROUP:
            outgoing[k] = value
            regroup(k)
        else:
            exchange(steps[place], k, value)

    rest = tuple(range(2, partner_levels))
    orders = [((0, 1) + rest, 0, first_grouped)]
    middle = first_grouped + chunks // 3
    orders.append(((1, REGROUP, 0) + rest, first_grouped, middle))
    orders.append(((REGROUP, 0, 1) + rest, middle, chunks))
    turns = max(last - first for _, first, last in orders)

    plan = []
    for number, (steps, _, _) in enumerate(orders):
        for place in range(len(steps) + 1):
            lag = sum(step != partner_levels - 1 for step in steps[:place])
            plan.append((lag, place, number))
    plan.sort()

    def turn(now, carry):
        for lag, place, number in plan:
            steps, first, last = orders[number]
            k = first + now - lag
            pl.when((k >= first) & (k < last))(functools.partial(stage, steps, place, k))
        return carry

    lax.fori_loop(0, turns + plan[-1][0], turn, 0)

    def finish_late(k, carry):
        for step in range(1, narrow):
            hand_over(step, k, True).wait()
        write_out(k, narrow_place).wait()
        return carry

    def finish(k, carry):
        for z in range(narrow):
            write_out(k, z).wait()
        return carry

    lax.fori_loop(first_grouped, chunks, finish, 0)
    lax.fori_loop(0, first_grouped, finish_late, 0)


def local(weights_in, medium_speed, target_order):
    wide = lax.axis_size("wide")
    narrow = lax.axis_size("narrow")
    codes, supers, tiles = weights_in.shape[:3]
    slots = tiles // narrow
    chunks = slots * (supers // SUPERS)
    partner_levels = wide.bit_length() - 1
    nodes = cheb_nodes().astype(np.float32)
    node_table = np.stack(
        [np.repeat(nodes[:, None], 128, axis=1), np.repeat(np.repeat(nodes, 16)[None], 8, axis=0)]
    )
    chunk_shape = (narrow, codes, SUPERS, 2, 8, 128)
    sizes = (wide, narrow, codes, supers, slots)
    scalars = pl.BlockSpec(memory_space=pltpu.SMEM)
    vectors = pl.BlockSpec(memory_space=pltpu.VMEM)
    anywhere = pl.BlockSpec(memory_space=pl.ANY)
    matrices = 2 * partner_levels + 4 * (4 - partner_levels)
    return pl.pallas_call(
        functools.partial(kernel, sizes),
        out_shape=jax.ShapeDtypeStruct(
            (codes, slots, supers * narrow) + weights_in.shape[3:], jnp.float32
        ),
        in_specs=[scalars, scalars, anywhere, anywhere, vectors],
        out_specs=anywhere,
        scratch_shapes=[
            pltpu.VMEM(weights_in.shape, jnp.float32),
            pltpu.VMEM((matrices, 2, 256, 256), jnp.bfloat16),
            pltpu.VMEM((chunks,) + chunk_shape, jnp.float32),
            pltpu.VMEM((chunks,) + chunk_shape, jnp.float32),
            pltpu.VMEM((partner_levels, chunks) + chunk_shape, jnp.float32),
            pltpu.VMEM((chunks - late_chunks(chunks),) + chunk_shape, jnp.float32),
            pltpu.SemaphoreType.DMA((codes, supers // SUPERS)),
            pltpu.SemaphoreType.DMA((matrices,)),
            pltpu.SemaphoreType.DMA((partner_levels, chunks)),
            pltpu.SemaphoreType.DMA((partner_levels, chunks)),
            pltpu.SemaphoreType.DMA((narrow - 1, chunks)),
            pltpu.SemaphoreType.DMA((narrow - 1, chunks)),
            pltpu.SemaphoreType.DMA((narrow, chunks)),
        ],
        compiler_params=pltpu.CompilerParams(
            collective_id=0, has_side_effects=True, vmem_limit_bytes=62 * 2**20
        ),
    )(
        target_order,
        medium_speed,
        weights_in,
        jnp.asarray(all_matrices(8 * narrow)),
        jnp.asarray(node_table),
    )


def solution(mesh):
    in_specs = (P("wide", "narrow", None, None, None, None), P(), P())
    out_specs = P("wide", "narrow", None, None, None, None)
    return jax.shard_map(local, mesh=mesh, in_specs=in_specs, out_specs=out_specs, check_vma=False)
```
